32 devices in a mesh: groups: 2 (over y), graph: 2 (over x), feat: 4 (over z), sub: 2 (over core).
Axes of the slice: x: 2, y: 2, z: 4, core: 2. Of those that a mesh axis runs over, the one named last changes fastest.
Arguments:
- node_features: bfloat16 [12288, 128], P(('groups', 'graph', 'feat', 'sub')), parts along dimension 0, may hold values from -6 to 6
- edge_features: bfloat16 [131072, 128], P(('groups', 'graph', 'feat', 'sub')), parts along dimension 0, may hold values from -6 to 6
- node_cotangent: bfloat16 [12288, 128], P(('groups', 'graph', 'feat', 'sub')), parts along dimension 0, may hold values from -6 to 6
- edge_cotangent: bfloat16 [131072, 128], P(('groups', 'graph', 'feat', 'sub')), parts along dimension 0, may hold values from -6 to 6
- senders: int32 [131072], P(('groups', 'graph', 'feat', 'sub')), parts along dimension 0, may hold values from 0 to 3199, as said below
- receivers: int32 [131072], P(('groups', 'graph', 'feat', 'sub')), parts along dimension 0, may hold values from 0 to 383
- send_rows: int32 [4, 2, 64], P(('groups', 'graph')), parts along dimension 0, may hold values from 0 to 3071
- live_edges: int32 [32], P(('groups', 'graph', 'feat', 'sub')), parts along dimension 0, may hold values from 1024 to 4096, as said below
- edge_in_weight: bfloat16 [384, 128], replicated, may hold values from -0.3125 to 0.3125
- edge_out_weight: bfloat16 [128, 128], replicated, may hold values from -0.5 to 0.5
- edge_bias: float32 [128], replicated, may hold values from -3 to 3
- edge_gain: float32 [128], replicated, may hold values from 0.25 to 1.75
- edge_shift: float32 [128], replicated, may hold values from -3 to 3
- node_in_weight: bfloat16 [256, 128], replicated, may hold values from -0.375 to 0.375
- node_out_weight: bfloat16 [128, 128], replicated, may hold values from -0.5 to 0.5
- node_bias: float32 [128], replicated, may hold values from -3 to 3
- node_gain: float32 [128], replicated, may hold values from 0.25 to 1.75
Outputs:
- node_grads: float32 [12288, 128], P(('groups', 'graph', 'feat', 'sub')), parts along dimension 0
- edge_grads: float32 [131072, 128], P(('groups', 'graph', 'feat', 'sub')), parts along dimension 0
- edge_in_grad: float32 [768, 128], P('groups'), parts along dimension 0
- edge_out_grad: float32 [256, 128], P('groups'), parts along dimension 0
- node_in_grad: float32 [512, 128], P('groups'), parts along dimension 0
- node_out_grad: float32 [256, 128], P('groups'), parts along dimension 0
- vector_grads: float32 [12, 128], P('groups'), parts along dimension 0
The draws below stay inside these ranges and needn't reach their ends.
There are 2 independent parts, one for each index of `groups`. The reference program is written for one: setup_inputs(seed, part) draws one part's arguments, and reference() takes and returns one part's arrays. A program takes and returns all parts, laid end to end along the dimension named above; an argument that names none is the same for every part. Nothing has to cross between parts.
Inputs may be any that keep to these rules, and one draw needn't show every extreme that they name: A sender below 3072 is a row of the edge's own partition; 3072 + q * 64 + k names the k-th row that partition q sends to it. Most senders lie among the rows of the edge's own device and the two slices beside it within the partition. `receivers`: a row of the edge's own device's nodes. send_rows[p, q, k] is the row of partition p's nodes that it sends to partition q as its k-th boundary row; rows may repeat. Slots from live_edges[d] on are padding; some device's slots are all used.
All inputs are finite; a program needn't handle non-finite values.
Results may differ from the reference program's by a relative error of at most 0.0066.
Values may be sent and summed in bfloat16 or wider, within the bound.
A program may use at most 128 MiB of HBM per device.

```python
import jax
import jax.numpy as jnp
from jax import lax

D = 128
NODE_DEV = 384
EDGE_DEV = 4096
HALO_PEER = 64
PARTITIONS = 2
SLICES = 8
NODE_PART = 3072
LOOKUP = 3200
NODES = 6144
DEVS = 16
EDGES = 65536
N_GRAPH = 2
N_FEAT = 4
N_SUB = 2


def draw_live_edges(key, part):
    key = jax.random.fold_in(key, 11)
    count_key, spot_key = jax.random.split(key)
    counts = jax.random.randint(count_key, (DEVS,), EDGE_DEV // 4, EDGE_DEV + 1)
    spot = jax.random.randint(spot_key, (), 0, DEVS)
    return jnp.where(jnp.arange(DEVS) == spot, EDGE_DEV, counts).astype(jnp.int32)


def draw_senders(key, part):
    key = jax.random.fold_in(key, 23)
    near_key, wide_key, halo_key, pick_key = jax.random.split(key, 4)
    slot = jnp.arange(EDGES, dtype=jnp.int32)
    slice_id = slot // EDGE_DEV % SLICES
    offset = jax.random.randint(near_key, (EDGES,), -NODE_DEV, 2 * NODE_DEV)
    near = (slice_id * NODE_DEV + offset + NODE_PART) % NODE_PART
    wide = jax.random.randint(wide_key, (EDGES,), 0, NODE_PART)
    halo = jax.random.randint(halo_key, (EDGES,), NODE_PART, LOOKUP)
    pick = jax.random.randint(pick_key, (EDGES,), 0, 10)
    chosen = jnp.where(pick < 8, near, jnp.where(pick == 8, wide, halo))
    chosen = jnp.where(slot == 0, 0, chosen)
    chosen = jnp.where(slot == 1, LOOKUP - 1, chosen)
    return chosen.astype(jnp.int32)


def touch_ends(values, key, smallest, high):
    extent = values.shape
    place = [jax.random.randint(jax.random.fold_in(key, axis), (), 0, extent[axis]) for axis in range(len(extent))]
    values = values.at[tuple(place)].set(smallest)
    longest = extent.index(max(extent))
    place[longest] = (place[longest] + 1) % extent[longest]
    return values.at[tuple(place)].set(high)


def level_of(stream_key, dims, pieces, least, largest):
    loudness = 1.0
    for dim, parts in pieces:
        heights = jax.random.uniform(jax.random.fold_in(jax.random.fold_in(stream_key, 6), dim), (parts,), jnp.float32, least / len(pieces), largest / len(pieces))
        loudness = loudness * jnp.repeat(jnp.exp(heights), dims[dim] // parts).reshape((-1,) + (1,) * (len(dims) - 1 - dim))
    return loudness


def bell_draw(key, extent, scale, bound, cuts=(), kind=jnp.bfloat16):
    values = scale * jax.random.normal(key, extent, jnp.float32)
    if cuts:
        values = values * level_of(key, extent, cuts, -0.22, 0.18)
    return jnp.clip(values, -bound, bound).astype(kind)


def setup_inputs(seed: int = 0, part: int = 0) -> dict:
    seeds = jax.random.split(jax.random.key(seed), 18)
    part_splits = jax.random.split(jax.random.fold_in(seeds[17], part), 18)
    return {
        "node_features": bell_draw(part_splits[0], (NODES, D), 1.0, 6.0, ((0, 16),)),
        "edge_features": bell_draw(part_splits[1], (EDGES, D), 1.0, 6.0, ((0, 16),)),
        "node_cotangent": bell_draw(part_splits[2], (NODES, D), 1.0, 6.0, ((0, 16),)),
        "edge_cotangent": bell_draw(part_splits[3], (EDGES, D), 1.0, 6.0, ((0, 16),)),
        "senders": draw_senders(jax.random.fold_in(jax.random.fold_in(seeds[17], part), 71), part),
        "receivers": touch_ends(jax.random.randint(part_splits[5], (EDGES,), 0, NODE_DEV), jax.random.fold_in(part_splits[5], 1), 0, NODE_DEV - 1).astype(jnp.int32),
        "send_rows": touch_ends(jax.random.randint(part_splits[6], (PARTITIONS, PARTITIONS, HALO_PEER), 0, NODE_PART), jax.random.fold_in(part_splits[6], 1), 0, NODE_PART - 1).astype(jnp.int32),
        "live_edges": draw_live_edges(jax.random.fold_in(jax.random.fold_in(seeds[17], part), 71), part),
        "edge_in_weight": bell_draw(seeds[8], (3 * D, D), (3 * D) ** -0.5, 0.3125),
        "edge_out_weight": bell_draw(seeds[9], (D, D), D ** -0.5, 0.5),
        "edge_bias": bell_draw(seeds[10], (D,), 0.5, 3.0, (), jnp.float32),
        "edge_gain": jnp.clip(1.0 + 0.15 * jax.random.normal(seeds[11], (D,), jnp.float32), 0.25, 1.75),
        "edge_shift": bell_draw(seeds[12], (D,), 0.5, 3.0, (), jnp.float32),
        "node_in_weight": bell_draw(seeds[13], (2 * D, D), (2 * D) ** -0.5, 0.375),
        "node_out_weight": bell_draw(seeds[14], (D, D), D ** -0.5, 0.5),
        "node_bias": bell_draw(seeds[15], (D,), 0.5, 3.0, (), jnp.float32),
        "node_gain": jnp.clip(1.0 + 0.15 * jax.random.normal(seeds[16], (D,), jnp.float32), 0.25, 1.75),
    }


epsilon = 1e-05

def norm_forward(output, gains, shifts):
    average = lax.optimization_barrier(jnp.mean(output, axis=-1, keepdims=True))
    centred = output - average
    inverse = lax.rsqrt(lax.optimization_barrier(jnp.mean(centred * centred, axis=-1, keepdims=True)) + epsilon)
    normed = centred * inverse
    return (normed * gains + shifts, normed, inverse)

def mlp_forward(inputs, w_in, biases, w_out, gains, shifts):
    preact = jnp.dot(inputs, w_in, preferred_element_type=jnp.float32) + biases
    hidden = (preact * jax.nn.sigmoid(preact)).astype(jnp.bfloat16)
    output = jnp.dot(hidden, w_out, preferred_element_type=jnp.float32)
    result, normed, inverse = norm_forward(output, gains, shifts)
    return (result, (preact, hidden, normed, inverse))

def mlp_backward(d_result, inputs, w_in, w_out, gains, stored):
    preact, hidden, normed, inverse = stored
    d_normed = d_result * gains
    d_output = inverse * (d_normed - lax.optimization_barrier(jnp.mean(d_normed, axis=-1, keepdims=True)) - normed * lax.optimization_barrier(jnp.mean(d_normed * normed, axis=-1, keepdims=True)))
    d_output_b = d_output.astype(jnp.bfloat16)
    grad_out = lax.dot_general(hidden, d_output_b, (((0,), (0,)), ((), ())), preferred_element_type=jnp.float32)
    d_hidden = lax.dot_general(d_output_b, w_out, (((1,), (1,)), ((), ())), preferred_element_type=jnp.float32)
    sigmoid = jax.nn.sigmoid(preact)
    d_preact = d_hidden * sigmoid * (1.0 + preact * (1.0 - sigmoid))
    d_preact_b = d_preact.astype(jnp.bfloat16)
    grad_in = lax.dot_general(inputs, d_preact_b, (((0,), (0,)), ((), ())), preferred_element_type=jnp.float32)
    d_inputs = lax.dot_general(d_preact_b, w_in, (((1,), (1,)), ((), ())), preferred_element_type=jnp.float32)
    vectors = jnp.stack([lax.optimization_barrier(jnp.sum(d_preact, axis=0)), lax.optimization_barrier(jnp.sum(d_result * normed, axis=0)), lax.optimization_barrier(jnp.sum(d_result, axis=0))])
    return (d_inputs, grad_in, grad_out, vectors)

def local_layer(lookup, node_rows, node_cot, edge_rows, edge_cot, sender_ids, receiver_ids, live_count, params):
    edge_in_weight, edge_out_weight, edge_bias, edge_gain, edge_shift, node_in_weight, node_out_weight, node_bias, node_gain = params
    edge_count = edge_rows.shape[0]
    node_count = node_rows.shape[0]
    width = node_rows.shape[1]
    live_mask = (jnp.arange(edge_count, dtype=jnp.int32) < live_count).astype(jnp.float32)[:, None]
    edge_inputs = jnp.concatenate([edge_rows, lookup[sender_ids], node_rows[receiver_ids]], axis=1)
    edge_update, edge_stored = mlp_forward(edge_inputs, edge_in_weight, edge_bias, edge_out_weight, edge_gain, edge_shift)
    edge_new = edge_rows.astype(jnp.float32) + live_mask * edge_update
    gathered = jax.ops.segment_sum(live_mask * edge_new, receiver_ids, num_segments=node_count)
    node_inputs = jnp.concatenate([node_rows, gathered.astype(jnp.bfloat16)], axis=1)
    node_update, node_stored = mlp_forward(node_inputs, node_in_weight, node_bias, node_out_weight, node_gain, jnp.zeros_like(node_gain))
    node_delta = node_cot.astype(jnp.float32)
    d_node_inputs, grad_node_in, grad_node_out, node_vectors = mlp_backward(node_delta, node_inputs, node_in_weight, node_out_weight, node_gain, node_stored)
    d_gathered = d_node_inputs[:, width:]
    d_edge_total = edge_cot.astype(jnp.float32) + live_mask * d_gathered[receiver_ids]
    d_edge_inputs, grad_edge_in, grad_edge_out, edge_vectors = mlp_backward(live_mask * d_edge_total, edge_inputs, edge_in_weight, edge_out_weight, edge_gain, edge_stored)
    edge_grads = d_edge_total + d_edge_inputs[:, :width]
    d_lookup = jax.ops.segment_sum(d_edge_inputs[:, width:2 * width], sender_ids, num_segments=lookup.shape[0])
    node_grads = node_delta + d_node_inputs[:, :width] + jax.ops.segment_sum(d_edge_inputs[:, 2 * width:], receiver_ids, num_segments=node_count)
    terms = (grad_edge_in, grad_edge_out, grad_node_in, grad_node_out, jnp.concatenate([edge_vectors, node_vectors], axis=0))
    return (node_grads, edge_grads, d_lookup, terms)

def reference(node_features, edge_features, node_cotangent, edge_cotangent, senders, receivers, send_rows, live_edges, edge_in_weight, edge_out_weight, edge_bias, edge_gain, edge_shift, node_in_weight, node_out_weight, node_bias, node_gain):
    params = (edge_in_weight, edge_out_weight, edge_bias, edge_gain, edge_shift, node_in_weight, node_out_weight, node_bias, node_gain)
    slices = N_FEAT * N_SUB
    node_part = NODE_DEV * slices
    parted = node_features.reshape(N_GRAPH, node_part, D)
    peers = jnp.arange(N_GRAPH, dtype=jnp.int32)[:, None]

    def device_step(carried, position):
        partials, gradients = carried
        part_id = position // slices
        own_rows = parted[part_id]
        rows_for_me = send_rows[:, part_id, :]
        boundary = parted[peers, rows_for_me].reshape(N_GRAPH * HALO_PEER, D)
        lookup = jnp.concatenate([own_rows, boundary], axis=0)
        node_start = (position * NODE_DEV).astype(jnp.int32)
        edge_start = (position * EDGE_DEV).astype(jnp.int32)
        node_rows = lax.dynamic_slice_in_dim(node_features, node_start, NODE_DEV, 0)
        node_cot = lax.dynamic_slice_in_dim(node_cotangent, node_start, NODE_DEV, 0)
        edge_rows = lax.dynamic_slice_in_dim(edge_features, edge_start, EDGE_DEV, 0)
        edge_cot = lax.dynamic_slice_in_dim(edge_cotangent, edge_start, EDGE_DEV, 0)
        sender_ids = lax.dynamic_slice_in_dim(senders, edge_start, EDGE_DEV, 0)
        receiver_ids = lax.dynamic_slice_in_dim(receivers, edge_start, EDGE_DEV, 0)
        node_grads, edge_grads, d_lookup, terms = local_layer(lookup, node_rows, node_cot, edge_rows, edge_cot, sender_ids, receiver_ids, live_edges[position], params)
        partials = partials.at[part_id].add(d_lookup[:node_part])
        partials = partials.at[peers, rows_for_me].add(d_lookup[node_part:].reshape(N_GRAPH, HALO_PEER, D))
        gradients = jax.tree.map(jnp.add, gradients, terms)
        return ((partials, gradients), (node_grads, edge_grads))
    start_grads = (jnp.zeros((3 * D, D), jnp.float32), jnp.zeros((D, D), jnp.float32), jnp.zeros((2 * D, D), jnp.float32), jnp.zeros((D, D), jnp.float32), jnp.zeros((6, D), jnp.float32))
    start = (jnp.zeros((N_GRAPH, node_part, D), jnp.float32), start_grads)
    (partials, gradients), (node_local, edge_local) = lax.scan(device_step, start, jnp.arange(N_GRAPH * slices, dtype=jnp.int32))
    node_total = node_local.reshape(-1, D) + partials.reshape(-1, D)
    edge_total = edge_local.reshape(-1, D)
    edge_scale = float(N_GRAPH * slices * EDGE_DEV) ** (-0.5)
    node_scale = float(N_GRAPH * node_part) ** (-0.5)
    row_scales = jnp.array([edge_scale] * 3 + [node_scale] * 3, jnp.float32)[:, None]
    return (node_total, edge_total, gradients[0] * edge_scale, gradients[1] * edge_scale, gradients[2] * node_scale, gradients[3] * node_scale, gradients[4] * row_scales)
```

```python
import functools

import jax
import jax.numpy as jnp
from jax import lax
from jax.experimental import pallas as pl
from jax.experimental.pallas import tpu as pltpu
from jax.sharding import PartitionSpec as P

epsilon = 1e-05
TILE = 512
F32 = jnp.float32
BF16 = jnp.bfloat16


def dot(a, b, ca=1, cb=0):
    return lax.dot_general(a, b, (((ca,), (cb,)), ((), ())), preferred_element_type=F32)


def sigmoid_of(x):
    return 0.5 * jnp.tanh(0.5 * x) + 0.5


def split(x):
    high = x.astype(BF16)
    low = (x - high.astype(F32)).astype(BF16)
    return jnp.concatenate([high, low], axis=1)


def mean(x):
    return jnp.mean(x, axis=-1, keepdims=True)


def forward(preact, w_out):
    hidden = (preact * sigmoid_of(preact)).astype(BF16)
    output = dot(hidden, w_out)
    centred = output - mean(output)
    inverse = lax.rsqrt(mean(centred * centred) + epsilon)
    return hidden, centred * inverse, inverse


def backward(r, preact, normed, inverse, w_out, gain):
    dn = r * gain
    d_output = inverse * (dn - mean(dn) - normed * mean(dn * normed))
    d_output_b = d_output.astype(BF16)
    d_hidden = dot(d_output_b, w_out, 1, 1)
    sig = sigmoid_of(preact)
    d_preact = d_hidden * sig * (1.0 + preact * (1.0 - sig))
    return d_output_b, d_preact


def down_rows(row):
    width = row.shape[1]
    return jnp.concatenate(
        [jnp.broadcast_to(row[:, c : c + 128], (128, 128)).T for c in range(0, width, 128)], axis=0
    )


def mark(hit):
    return jnp.where(hit, 1.0, 0.0).astype(BF16)


def layer_kernel(
    part_ref,
    halo_ref,
    node_ref,
    ncot_ref,
    ef_ref,
    ec_ref,
    snd_ref,
    rcv_ref,
    live_ref,
    ew1_ref,
    ew2_ref,
    evec_ref,
    nw1_ref,
    nw2_ref,
    nvec_ref,
    edge_out,
    node_out,
    sums_out,
    halo_out,
    terms_out,
    table,
    pair_table,
    slots_r,
    others,
    preacts,
    hiddens,
    normeds,
    inverses,
    gathered,
    acc,
    acc_rh,
):
    part_rows, width = part_ref.shape
    nodes = node_ref.shape[0]
    halos = halo_ref.shape[0]
    rows = table.shape[0]
    groups = part_rows // rows
    tiles = snd_ref.shape[0]
    live = live_ref[0]

    for g in range(groups):
        table[:, g * width : (g + 1) * width] = part_ref[g * rows : (g + 1) * rows, :]
    pair_table[0:nodes, 0:width] = node_ref[...]
    pair_table[0:nodes, width:] = jnp.zeros((nodes, width), BF16)
    pair_table[nodes:, 0:width] = jnp.zeros((halos, width), BF16)
    pair_table[nodes:, width:] = halo_ref[...]
    gathered[...] = jnp.zeros_like(gathered)
    acc[...] = jnp.zeros_like(acc)
    acc_rh[...] = jnp.zeros_like(acc_rh)
    terms_out[...] = jnp.zeros_like(terms_out)

    lane = lax.broadcasted_iota(jnp.int32, (TILE, 128), 1)
    deep = lax.broadcasted_iota(jnp.int32, (TILE, 128), 0)

    def group_of(s):
        group = jnp.zeros_like(s)
        for g in range(1, groups + 1):
            group = group + jnp.where(s >= g * rows, 1, 0)
        return group

    def ahead(i, _):
        here = pl.ds(pl.multiple_of(i * TILE, TILE), TILE)
        snd = snd_ref[i]
        s = down_rows(snd)
        r = down_rows(rcv_ref[i])
        group = group_of(s)
        low = s - group * rows
        far = s - part_rows
        low_hot = jnp.concatenate([mark(low == lane + j) for j in range(0, rows, 128)], axis=1)
        r_hot = jnp.concatenate([mark(r == lane + j) for j in range(0, nodes, 128)], axis=1)
        far_hot = jnp.concatenate([mark(far == lane + j) for j in range(0, halos, 128)], axis=1)
        slots_r[here, :] = r_hot
        picked = dot(low_hot, table[...])
        both = dot(jnp.concatenate([r_hot, far_hot], axis=1), pair_table[...])
        sent = both[:, width:]
        for g in range(groups):
            sent = jnp.where(group == g, picked[:, g * width : (g + 1) * width], sent)
        other = jnp.concatenate([sent.astype(BF16), both[:, :width].astype(BF16)], axis=1)
        others[here, :] = other
        ef = ef_ref[here, :]
        preact = dot(jnp.concatenate([ef, other], axis=1), ew1_ref[...]) + evec_ref[0:1, :]
        hidden, normed, inverse = forward(preact, ew2_ref[...])
        preacts[here, :] = preact
        hiddens[here, :] = hidden
        normeds[here, :] = normed
        inverses[here, :] = jnp.broadcast_to(inverse, (TILE, width))
        new = ef.astype(F32) + normed * evec_ref[1:2, :] + evec_ref[2:3, :]
        new = jnp.where(deep + i * TILE < live, new, 0.0)
        gathered[...] += dot(r_hot, split(new), 0, 0)
        return 0

    lax.fori_loop(0, tiles, ahead, 0)

    whole = gathered[:, :width] + gathered[:, width:]
    node_inputs = jnp.concatenate([node_ref[...], whole.astype(BF16)], axis=1)
    preact = dot(node_inputs, nw1_ref[...]) + nvec_ref[0:1, :]
    hidden, normed, inverse = forward(preact, nw2_ref[...])
    r = ncot_ref[...].astype(F32)
    d_output_b, d_preact = backward(r, preact, normed, inverse, nw2_ref[...], nvec_ref[1:2, :])
    d_preact_b = d_preact.astype(BF16)
    e1 = 3 * width
    e2 = e1 + width
    n1 = e2 + 2 * width
    n2 = n1 + width
    terms_out[e2:n1, :] = dot(node_inputs, d_preact_b, 0, 0)
    terms_out[n1:n2, :] = dot(hidden, d_output_b, 0, 0)
    terms_out[n2 + 3 : n2 + 4, :] = jnp.sum(d_preact, axis=0, keepdims=True)
    terms_out[n2 + 4 : n2 + 5, :] = jnp.sum(r * normed, axis=0, keepdims=True)
    terms_out[n2 + 5 : n2 + 6, :] = jnp.sum(r, axis=0, keepdims=True)
    d_inputs = dot(d_preact_b, nw1_ref[...], 1, 1)
    node_out[...] = r + d_inputs[:, :width]
    spread = split(d_inputs[:, width:])

    low_deep = lax.broadcasted_iota(jnp.int32, (rows, TILE), 0)
    node_deep = lax.broadcasted_iota(jnp.int32, (nodes, TILE), 0)
    halo_deep = lax.broadcasted_iota(jnp.int32, (halos, TILE), 0)

    def back(i, carried):
        sum_b, sum_g, sum_s = carried
        here = pl.ds(pl.multiple_of(i * TILE, TILE), TILE)
        snd = snd_ref[i]
        rcv = rcv_ref[i]
        group = group_of(snd)
        low_hot = mark(low_deep == snd - group * rows)
        r_hot = mark(node_deep == rcv)
        far_hot = mark(halo_deep == snd - part_rows)
        alive = deep + i * TILE < live
        dg = dot(slots_r[here, :], spread)
        dg = dg[:, :width] + dg[:, width:]
        total = ec_ref[here, :].astype(F32) + jnp.where(alive, dg, 0.0)
        r = jnp.where(alive, total, 0.0)
        normed = normeds[here, :]
        d_output_b, d_preact = backward(
            r, preacts[here, :], normed, inverses[here, :], ew2_ref[...], evec_ref[1:2, :]
        )
        d_preact_b = d_preact.astype(BF16)
        edge_out[here, :] = total + dot(d_preact_b, ew1_ref[0:width, :], 1, 1)
        inputs = jnp.concatenate([ef_ref[here, :], others[here, :]], axis=1)
        terms_out[0:e1, :] += dot(inputs, d_preact_b, 0, 0)
        terms_out[e1:e2, :] += dot(hiddens[here, :], d_output_b, 0, 0)
        down = group_of(down_rows(snd))
        zero = jnp.zeros_like(d_preact)
        placed = jnp.concatenate(
            [jnp.where(down == g, d_preact, zero).astype(BF16) for g in range(groups)], axis=1
        )
        acc[...] += dot(low_hot, placed)
        acc_rh[...] += dot(jnp.concatenate([r_hot, far_hot], axis=0), d_preact_b)
        return (
            sum_b + jnp.sum(d_preact, axis=0, keepdims=True),
            sum_g + jnp.sum(r * normed, axis=0, keepdims=True),
            sum_s + jnp.sum(r, axis=0, keepdims=True),
        )

    none = jnp.zeros((1, width), F32)
    sum_b, sum_g, sum_s = lax.fori_loop(0, tiles, back, (none, none, none))
    terms_out[n2 : n2 + 1, :] = sum_b
    terms_out[n2 + 1 : n2 + 2, :] = sum_g
    terms_out[n2 + 2 : n2 + 3, :] = sum_s
    for g in range(groups):
        sums_out[g * rows : (g + 1) * rows, :] = acc[:, g * width : (g + 1) * width].astype(BF16)
    halo_out[...] = acc_rh[nodes:, :].astype(BF16)
    node_out[...] += dot(acc_rh[0:nodes, :].astype(BF16), ew1_ref[2 * width :, :], 1, 1)


def layer(part, halo, node_rows, node_cot, edge_rows, edge_cot, senders, receivers, live, params):
    ew1, ew2, eb, eg, es, nw1, nw2, nb, ng = params
    edges, width = edge_rows.shape
    nodes = node_rows.shape[0]
    halos = halo.shape[0]
    rows = 2 * nodes
    groups = part.shape[0] // rows
    tiles = edges // TILE
    evec = jnp.stack([eb, eg, es])
    nvec = jnp.stack([nb, ng])
    terms = 7 * width + 8
    vmem = pl.BlockSpec(memory_space=pltpu.VMEM)
    smem = pl.BlockSpec(memory_space=pltpu.SMEM)
    return pl.pallas_call(
        layer_kernel,
        out_shape=(
            jax.ShapeDtypeStruct((edges, width), F32),
            jax.ShapeDtypeStruct((nodes, width), F32),
            jax.ShapeDtypeStruct(part.shape, BF16),
            jax.ShapeDtypeStruct(halo.shape, BF16),
            jax.ShapeDtypeStruct((terms, width), F32),
        ),
        in_specs=[vmem] * 8 + [smem] + [vmem] * 6,
        out_specs=[vmem] * 5,
        scratch_shapes=[
            pltpu.VMEM((rows, groups * width), BF16),
            pltpu.VMEM((nodes + halos, 2 * width), BF16),
            pltpu.VMEM((edges, nodes), BF16),
            pltpu.VMEM((edges, 2 * width), BF16),
            pltpu.VMEM((edges, width), F32),
            pltpu.VMEM((edges, width), BF16),
            pltpu.VMEM((edges, width), F32),
            pltpu.VMEM((edges, width), F32),
            pltpu.VMEM((nodes, 2 * width), F32),
            pltpu.VMEM((rows, groups * width), F32),
            pltpu.VMEM((nodes + halos, width), F32),
        ],
        compiler_params=pltpu.CompilerParams(vmem_limit_bytes=56 * 2**20),
        cost_estimate=pl.CostEstimate(
            flops=2 * edges * width * 10000, bytes_accessed=8 * 2**20, transcendentals=0
        ),
    )(
        part,
        halo,
        node_rows,
        node_cot,
        edge_rows,
        edge_cot,
        senders.reshape(tiles, 1, TILE),
        receivers.reshape(tiles, 1, TILE),
        live,
        ew1,
        ew2,
        evec,
        nw1,
        nw2,
        nvec,
    )


def per_device(
    node_features,
    edge_features,
    node_cotangent,
    edge_cotangent,
    senders,
    receivers,
    send_rows,
    live_edges,
    *params,
):
    slices = lax.axis_size(("feat", "sub"))
    partition = lax.all_gather(node_features, ("feat", "sub"), axis=0, tiled=True)
    node_part, width = partition.shape
    row_lists = send_rows[0]
    peers, per_peer = row_lists.shape
    outgoing = partition[row_lists]
    arrived = lax.all_to_all(outgoing, "graph", split_axis=0, concat_axis=0, tiled=True)
    edge_grads, node_base, sums, halo_sums, terms = layer(
        partition,
        arrived.reshape(peers * per_peer, width),
        node_features,
        node_cotangent,
        edge_features,
        edge_cotangent,
        senders,
        receivers,
        live_edges,
        params,
    )
    summed = lax.psum(terms, ("graph", "feat", "sub"))
    returned = lax.all_to_all(
        halo_sums.reshape(peers, per_peer, width), "graph", split_axis=0, concat_axis=0, tiled=True
    )
    hot = (
        row_lists.reshape(1, -1) == jnp.arange(node_part, dtype=jnp.int32)[:, None]
    ).astype(BF16)
    partial_value = sums.astype(F32) + dot(hot, returned.reshape(-1, width))
    own = lax.psum_scatter(
        partial_value.astype(BF16), ("feat", "sub"), scatter_dimension=0, tiled=True
    )
    node_total = node_base + dot(own, params[0][width : 2 * width], 1, 1)
    device_count = lax.axis_size("graph") * slices
    edge_scale = float(device_count * edge_features.shape[0]) ** (-0.5)
    node_scale = float(device_count * node_features.shape[0]) ** (-0.5)
    row_scales = jnp.array([edge_scale] * 3 + [node_scale] * 3, F32)[:, None]
    e1, e2, n1, n2 = 3 * width, 4 * width, 6 * width, 7 * width
    return (
        node_total,
        edge_grads,
        summed[:e1] * edge_scale,
        summed[e1:e2] * edge_scale,
        summed[e2:n1] * node_scale,
        summed[n1:n2] * node_scale,
        summed[n2 : n2 + 6] * row_scales,
    )


def solution(mesh):
    everywhere = ("groups", "graph", "feat", "sub")
    in_specs = (
        P(everywhere, None),
        P(everywhere, None),
        P(everywhere, None),
        P(everywhere, None),
        P(everywhere),
        P(everywhere),
        P(("groups", "graph"), None, None),
        P(everywhere),
    ) + (P(),) * 9
    out_specs = (
        P(everywhere, None),
        P(everywhere, None),
    ) + (P("groups", None),) * 5
    return jax.shard_map(
        per_device, mesh=mesh, in_specs=in_specs, out_specs=out_specs, check_vma=False
    )
```

```python
import functools

import jax
import jax.numpy as jnp
from jax import lax
from jax.experimental import pallas as pl
from jax.experimental.pallas import tpu as pltpu
from jax.sharding import PartitionSpec as P

epsilon = 1e-05
TILE = 512
F32 = jnp.float32
BF16 = jnp.bfloat16


def dot(a, b, ca=1, cb=0):
    return lax.dot_general(a, b, (((ca,), (cb,)), ((), ())), preferred_element_type=F32)


def sigmoid_of(x):
    return 0.5 * jnp.tanh(0.5 * x) + 0.5


def split(x):
    high = x.astype(BF16)
    low = (x - high.astype(F32)).astype(BF16)
    return jnp.concatenate([high, low], axis=1)


def mean(x):
    return jnp.mean(x, axis=-1, keepdims=True)


def forward(preact, w_out):
    hidden = (preact * sigmoid_of(preact)).astype(BF16)
    output = dot(hidden, w_out)
    centred = output - mean(output)
    inverse = lax.rsqrt(mean(centred * centred) + epsilon)
    return hidden, centred * inverse, inverse


def backward(r, preact, normed, inverse, w_out, gain):
    dn = r * gain
    d_output = inverse * (dn - mean(dn) - normed * mean(dn * normed))
    d_output_b = d_output.astype(BF16)
    d_hidden = dot(d_output_b, w_out, 1, 1)
    sig = sigmoid_of(preact)
    d_preact = d_hidden * sig * (1.0 + preact * (1.0 - sig))
    return d_output_b, d_preact


def down_rows(row):
    width = row.shape[1]
    return jnp.concatenate(
        [jnp.broadcast_to(row[:, c : c + 128], (128, 128)).T for c in range(0, width, 128)], axis=0
    )


def mark(hit):
    return jnp.where(hit, 1.0, 0.0).astype(BF16)


def layer_kernel(
    part_ref,
    halo_ref,
    node_ref,
    ncot_ref,
    ef_ref,
    ec_ref,
    snd_ref,
    rcv_ref,
    live_ref,
    ew1_ref,
    ew2_ref,
    evec_ref,
    nw1_ref,
    nw2_ref,
    nvec_ref,
    edge_out,
    node_out,
    sums_out,
    halo_out,
    terms_out,
    table,
    pair_table,
    slots_r,
    others,
    preacts,
    hiddens,
    normeds,
    inverses,
    gathered,
    acc,
    acc_rh,
):
    slots, nodes, width = part_ref.shape
    part_rows = slots * nodes
    halos = halo_ref.shape[0]
    rows = table.shape[0]
    groups = part_rows // rows
    tiles = snd_ref.shape[0]
    live = live_ref[0]

    for g in range(groups):
        for k in range(rows // nodes):
            table[k * nodes : (k + 1) * nodes, g * width : (g + 1) * width] = part_ref[
                g * (rows // nodes) + k
            ]
    pair_table[0:nodes, 0:width] = node_ref[...]
    pair_table[0:nodes, width:] = jnp.zeros((nodes, width), BF16)
    pair_table[nodes:, 0:width] = jnp.zeros((halos, width), BF16)
    pair_table[nodes:, width:] = halo_ref[...]
    gathered[...] = jnp.zeros_like(gathered)
    acc[...] = jnp.zeros_like(acc)
    acc_rh[...] = jnp.zeros_like(acc_rh)
    terms_out[...] = jnp.zeros_like(terms_out)

    lane = lax.broadcasted_iota(jnp.int32, (TILE, 128), 1)
    deep = lax.broadcasted_iota(jnp.int32, (TILE, 128), 0)

    def group_of(s):
        group = jnp.zeros_like(s)
        for g in range(1, groups + 1):
            group = group + jnp.where(s >= g * rows, 1, 0)
        return group

    def ahead(i, _):
        here = pl.ds(pl.multiple_of(i * TILE, TILE), TILE)
        snd = snd_ref[i]
        s = down_rows(snd)
        r = down_rows(rcv_ref[i])
        group = group_of(s)
        low = s - group * rows
        far = s - part_rows
        low_hot = jnp.concatenate([mark(low == lane + j) for j in range(0, rows, 128)], axis=1)
        r_hot = jnp.concatenate([mark(r == lane + j) for j in range(0, nodes, 128)], axis=1)
        far_hot = jnp.concatenate([mark(far == lane + j) for j in range(0, halos, 128)], axis=1)
        slots_r[here, :] = r_hot
        picked = dot(low_hot, table[...])
        both = dot(jnp.concatenate([r_hot, far_hot], axis=1), pair_table[...])
        sent = both[:, width:]
        for g in range(groups):
            sent = jnp.where(group == g, picked[:, g * width : (g + 1) * width], sent)
        other = jnp.concatenate([sent.astype(BF16), both[:, :width].astype(BF16)], axis=1)
        others[here, :] = other
        ef = ef_ref[here, :]
        preact = dot(jnp.concatenate([ef, other], axis=1), ew1_ref[...]) + evec_ref[0:1, :]
        hidden, normed, inverse = forward(preact, ew2_ref[...])
        preacts[here, :] = preact
        hiddens[here, :] = hidden
        normeds[here, :] = normed
        inverses[here, :] = jnp.broadcast_to(inverse, (TILE, width))
        new = ef.astype(F32) + normed * evec_ref[1:2, :] + evec_ref[2:3, :]
        new = jnp.where(deep + i * TILE < live, new, 0.0)
        gathered[...] += dot(r_hot, split(new), 0, 0)
        return 0

    lax.fori_loop(0, tiles, ahead, 0)

    whole = gathered[:, :width] + gathered[:, width:]
    node_inputs = jnp.concatenate([node_ref[...], whole.astype(BF16)], axis=1)
    preact = dot(node_inputs, nw1_ref[...]) + nvec_ref[0:1, :]
    hidden, normed, inverse = forward(preact, nw2_ref[...])
    r = ncot_ref[...].astype(F32)
    d_output_b, d_preact = backward(r, preact, normed, inverse, nw2_ref[...], nvec_ref[1:2, :])
    d_preact_b = d_preact.astype(BF16)
    e1 = 3 * width
    e2 = e1 + width
    n1 = e2 + 2 * width
    n2 = n1 + width
    terms_out[e2:n1, :] = dot(node_inputs, d_preact_b, 0, 0)
    terms_out[n1:n2, :] = dot(hidden, d_output_b, 0, 0)
    terms_out[n2 + 3 : n2 + 4, :] = jnp.sum(d_preact, axis=0, keepdims=True)
    terms_out[n2 + 4 : n2 + 5, :] = jnp.sum(r * normed, axis=0, keepdims=True)
    terms_out[n2 + 5 : n2 + 6, :] = jnp.sum(r, axis=0, keepdims=True)
    d_inputs = dot(d_preact_b, nw1_ref[...], 1, 1)
    node_out[...] = r + d_inputs[:, :width]
    spread = split(d_inputs[:, width:])

    low_deep = lax.broadcasted_iota(jnp.int32, (rows, TILE), 0)
    node_deep = lax.broadcasted_iota(jnp.int32, (nodes, TILE), 0)
    halo_deep = lax.broadcasted_iota(jnp.int32, (halos, TILE), 0)

    def back(i, carried):
        sum_b, sum_g, sum_s = carried
        here = pl.ds(pl.multiple_of(i * TILE, TILE), TILE)
        snd = snd_ref[i]
        rcv = rcv_ref[i]
        group = group_of(snd)
        low_hot = mark(low_deep == snd - group * rows)
        r_hot = mark(node_deep == rcv)
        far_hot = mark(halo_deep == snd - part_rows)
        alive = deep + i * TILE < live
        dg = dot(slots_r[here, :], spread)
        dg = dg[:, :width] + dg[:, width:]
        total = ec_ref[here, :].astype(F32) + jnp.where(alive, dg, 0.0)
        r = jnp.where(alive, total, 0.0)
        normed = normeds[here, :]
        d_output_b, d_preact = backward(
            r, preacts[here, :], normed, inverses[here, :], ew2_ref[...], evec_ref[1:2, :]
        )
        d_preact_b = d_preact.astype(BF16)
        edge_out[here, :] = total + dot(d_preact_b, ew1_ref[0:width, :], 1, 1)
        inputs = jnp.concatenate([ef_ref[here, :], others[here, :]], axis=1)
        terms_out[0:e1, :] += dot(inputs, d_preact_b, 0, 0)
        terms_out[e1:e2, :] += dot(hiddens[here, :], d_output_b, 0, 0)
        down = group_of(down_rows(snd))
        zero = jnp.zeros_like(d_preact)
        placed = jnp.concatenate(
            [jnp.where(down == g, d_preact, zero).astype(BF16) for g in range(groups)], axis=1
        )
        acc[...] += dot(low_hot, placed)
        acc_rh[...] += dot(jnp.concatenate([r_hot, far_hot], axis=0), d_preact_b)
        return (
            sum_b + jnp.sum(d_preact, axis=0, keepdims=True),
            sum_g + jnp.sum(r * normed, axis=0, keepdims=True),
            sum_s + jnp.sum(r, axis=0, keepdims=True),
        )

    none = jnp.zeros((1, width), F32)
    sum_b, sum_g, sum_s = lax.fori_loop(0, tiles, back, (none, none, none))
    terms_out[n2 : n2 + 1, :] = sum_b
    terms_out[n2 + 1 : n2 + 2, :] = sum_g
    terms_out[n2 + 2 : n2 + 3, :] = sum_s
    for g in range(groups):
        for k in range(rows // nodes):
            sums_out[g * (rows // nodes) + k] = acc[
                k * nodes : (k + 1) * nodes, g * width : (g + 1) * width
            ].astype(BF16)
    halo_out[...] = acc_rh[nodes:, :].astype(BF16)
    node_out[...] += dot(acc_rh[0:nodes, :].astype(BF16), ew1_ref[2 * width :, :], 1, 1)


def layer(part, halo, node_rows, node_cot, edge_rows, edge_cot, senders, receivers, live, params, terms):
    ew1, ew2, eb, eg, es, nw1, nw2, nb, ng = params
    edges, width = edge_rows.shape
    nodes = node_rows.shape[0]
    halos = halo.shape[0]
    rows = 2 * nodes
    groups = part.shape[0] * part.shape[1] // rows
    tiles = edges // TILE
    evec = jnp.stack([eb, eg, es])
    nvec = jnp.stack([nb, ng])
    vmem = pl.BlockSpec(memory_space=pltpu.VMEM)
    smem = pl.BlockSpec(memory_space=pltpu.SMEM)
    return pl.pallas_call(
        layer_kernel,
        out_shape=(
            jax.ShapeDtypeStruct((edges, width), F32),
            jax.ShapeDtypeStruct((nodes, width), F32),
            jax.ShapeDtypeStruct(part.shape, BF16),
            jax.ShapeDtypeStruct(halo.shape, BF16),
            jax.ShapeDtypeStruct((terms, width), F32),
        ),
        in_specs=[vmem] * 8 + [smem] + [vmem] * 6,
        out_specs=[vmem] * 5,
        scratch_shapes=[
            pltpu.VMEM((rows, groups * width), BF16),
            pltpu.VMEM((nodes + halos, 2 * width), BF16),
            pltpu.VMEM((edges, nodes), BF16),
            pltpu.VMEM((edges, 2 * width), BF16),
            pltpu.VMEM((edges, width), F32),
            pltpu.VMEM((edges, width), BF16),
            pltpu.VMEM((edges, width), F32),
            pltpu.VMEM((edges, width), F32),
            pltpu.VMEM((nodes, 2 * width), F32),
            pltpu.VMEM((rows, groups * width), F32),
            pltpu.VMEM((nodes + halos, width), F32),
        ],
        compiler_params=pltpu.CompilerParams(vmem_limit_bytes=56 * 2**20),
        cost_estimate=pl.CostEstimate(
            flops=2 * edges * width * 10000, bytes_accessed=8 * 2**20, transcendentals=0
        ),
    )(
        part,
        halo,
        node_rows,
        node_cot,
        edge_rows,
        edge_cot,
        senders.reshape(tiles, 1, TILE),
        receivers.reshape(tiles, 1, TILE),
        live,
        ew1,
        ew2,
        evec,
        nw1,
        nw2,
        nvec,
    )


def greet(partners):
    barrier = pltpu.get_barrier_semaphore()
    for partner in partners:
        pl.semaphore_signal(
            barrier, inc=1, device_id=partner, device_id_type=pl.DeviceIdType.MESH
        )
    pl.semaphore_wait(barrier, len(partners))


def push(src, dst, send, recv, partner):
    return pltpu.make_async_remote_copy(
        src_ref=src,
        dst_ref=dst,
        send_sem=send,
        recv_sem=recv,
        device_id=partner,
        device_id_type=pl.DeviceIdType.MESH,
    )


def around(axis, count):
    me = lax.axis_index(axis)
    return [{axis: lax.rem(me + off, count)} for off in range(1, count)]


def gather_kernel(
    peers, feats, node_ref, rows_ref, part_ref, halo_ref, picked,
    feat_send, feat_recv, sub_send, sub_recv, graph_send, graph_recv
):
    p = lax.axis_index("graph")
    f = lax.axis_index("feat")
    c = lax.axis_index("sub")
    sibling = {"sub": 1 - c}
    nodes = node_ref.shape[0]
    halos = rows_ref.shape[1]
    per = halos // peers
    greet([sibling] + around("feat", feats) + around("graph", peers))
    mine = 2 * f + c
    started = []

    def go(copy):
        copy.start()
        started.append(copy)

    for off in range(feats - 1, 0, -1):
        to = {"feat": lax.rem(f + off, feats)}
        go(push(node_ref, part_ref.at[mine], feat_send.at[off], feat_recv.at[off], to))
    go(push(node_ref, part_ref.at[mine], sub_send.at[0], sub_recv.at[0], sibling))
    part_ref[mine] = node_ref[...]
    for off in range(1, feats):
        source = lax.rem(f + feats - off, feats)
        slot = part_ref.at[2 * source + c]
        push(node_ref, slot, feat_send.at[off], feat_recv.at[off], sibling).wait_recv()
        go(push(slot, slot, sub_send.at[off], sub_recv.at[off], sibling))
    for off in range(feats):
        source = lax.rem(f + feats - off, feats)
        slot = part_ref.at[2 * source + 1 - c]
        push(slot, slot, sub_send.at[off], sub_recv.at[off], sibling).wait_recv()
    deep = lax.broadcasted_iota(jnp.int32, (nodes, halos), 0)
    listed = rows_ref[...]
    chosen = jnp.zeros((halos, node_ref.shape[1]), F32)
    for slot in range(2 * feats):
        chosen = chosen + dot(mark(deep + slot * nodes == listed), part_ref[slot], 0, 0)
    chosen = chosen.astype(BF16)
    for q in range(peers):
        picked[q] = chosen[q * per : (q + 1) * per, :]
    for off in range(1, peers):
        to = lax.rem(p + off, peers)
        go(
            push(
                picked.at[to], halo_ref.at[p], graph_send.at[off], graph_recv.at[off],
                {"graph": to},
            )
        )
    halo_ref[p] = picked[p]
    for off in range(1, peers):
        source = lax.rem(p + peers - off, peers)
        push(
            picked.at[0], halo_ref.at[source], graph_send.at[off], graph_recv.at[off], sibling
        ).wait_recv()
    for copy in started:
        copy.wait_send()


def gather(node_rows, row_lists, feats):
    nodes, width = node_rows.shape
    peers, per = row_lists.shape
    vmem = pl.BlockSpec(memory_space=pltpu.VMEM)
    dma = pltpu.SemaphoreType.DMA
    return pl.pallas_call(
        functools.partial(gather_kernel, peers, feats),
        out_shape=(
            jax.ShapeDtypeStruct((2 * feats, nodes, width), BF16),
            jax.ShapeDtypeStruct((peers, per, width), BF16),
        ),
        in_specs=[vmem] * 2,
        out_specs=[vmem] * 2,
        scratch_shapes=[
            pltpu.VMEM((peers, per, width), BF16),
            dma((feats,)),
            dma((feats,)),
            dma((feats,)),
            dma((feats,)),
            dma((peers,)),
            dma((peers,)),
        ],
        compiler_params=pltpu.CompilerParams(
            collective_id=0, has_side_effects=True, vmem_limit_bytes=32 * 2**20
        ),
    )(node_rows, row_lists.reshape(1, peers * per))


def reduce_kernel(
    peers, feats, edge_scale, node_scale,
    sums_ref, halo_ref, rows_ref, terms_ref, base_ref, w1_ref,
    node_out, ein_out, eout_out, nin_out, nout_out, vec_out,
    narrow, first, second, third, mid, late, onward, result,
    returned, paired, ready, arrived,
    halo_send, halo_recv, pair_send, pair_recv, feat_send, feat_recv,
    t_sub_send, t_sub_recv, t_graph_send, t_graph_recv, t_feat_send, t_feat_recv,
    g_sub_send, g_sub_recv, g_graph_send, g_graph_recv, g_feat_send, g_feat_recv
):
    p = lax.axis_index("graph")
    f = lax.axis_index("feat")
    c = lax.axis_index("sub")
    sibling = {"sub": 1 - c}
    slots, nodes, width = sums_ref.shape
    halos = rows_ref.shape[1]
    per = halos // peers
    across = [{"graph": to["graph"], "sub": 1 - c} for to in around("graph", peers)]
    greet([sibling] + around("feat", feats) + around("graph", peers) + across)
    started = []

    def go(copy):
        copy.start()
        started.append(copy)

    for off in range(1, peers):
        to = lax.rem(p + off, peers)
        for swap, core in enumerate((c, 1 - c)):
            go(
                push(
                    halo_ref.at[to], returned.at[c, p],
                    halo_send.at[swap, off], halo_recv.at[swap, off],
                    {"graph": to, "sub": core},
                )
            )
    go(push(halo_ref.at[p], returned.at[c, p], halo_send.at[1, 0], halo_recv.at[1, 0], sibling))
    narrow[...] = terms_ref[...].astype(BF16)
    go(push(narrow.at[1 - c], first, t_sub_send, t_sub_recv, sibling))
    for off in range(feats - 1, -1, -1):
        to = lax.rem(f + off, feats)
        go(
            push(
                sums_ref.at[2 * to + 1 - c], paired.at[to], pair_send.at[to], pair_recv.at[to],
                sibling,
            )
        )
    returned[c, p] = halo_ref[p]

    push(first, first, t_sub_send, t_sub_recv, sibling).wait_recv()
    mid[...] = (terms_ref[c] + first[...].astype(F32)).astype(BF16)
    for off in range(1, peers):
        to = lax.rem(p + off, peers)
        go(
            push(
                mid.at[to], second.at[p], t_graph_send.at[off], t_graph_recv.at[off],
                {"graph": to},
            )
        )

    for swap, core in enumerate((c, 1 - c)):
        for off in range(1 - swap, peers):
            piece = returned.at[core, lax.rem(p + peers - off, peers)]
            push(
                piece, piece, halo_send.at[swap, off], halo_recv.at[swap, off], sibling
            ).wait_recv()
    boundary = returned[...].reshape(2 * halos, width)
    deep = lax.broadcasted_iota(jnp.int32, (nodes, 2 * halos), 0)
    listed = jnp.concatenate([rows_ref[...], rows_ref[...]], axis=1)

    def joined(owner):
        push(
            paired.at[owner], paired.at[owner], pair_send.at[owner], pair_recv.at[owner], sibling
        ).wait_recv()
        place = 2 * owner + c
        extra = dot(mark(deep + place * nodes == listed), boundary)
        return sums_ref[place].astype(F32) + paired[owner].astype(F32) + extra

    for off in range(feats - 1, 0, -1):
        to = lax.rem(f + off, feats)
        ready[to] = joined(to).astype(BF16)
        go(
            push(
                ready.at[to], arrived.at[f], feat_send.at[off], feat_recv.at[off], {"feat": to}
            )
        )
    own = joined(f)

    total = terms_ref[c, p] + first[p].astype(F32)
    for off in range(1, peers):
        source = lax.rem(p + peers - off, peers)
        push(
            second.at[source], second.at[source], t_graph_send.at[off], t_graph_recv.at[off],
            sibling,
        ).wait_recv()
        total = total + second[source].astype(F32)
    late[...] = total
    onward[...] = total.astype(BF16)
    for off in range(feats - 1, 0, -1):
        to = lax.rem(f + off, feats)
        go(
            push(
                onward.at[to], third.at[f], t_feat_send.at[off], t_feat_recv.at[off],
                {"feat": to},
            )
        )
    total = late[f]
    for off in range(1, feats):
        source = lax.rem(f + feats - off, feats)
        push(
            third.at[source], third.at[source], t_feat_send.at[off], t_feat_recv.at[off], sibling
        ).wait_recv()
        total = total + third[source].astype(F32)
    result[c, p, f] = total.astype(BF16)
    for off in range(1, feats):
        to = lax.rem(f + off, feats)
        piece = result.at[c, p, f]
        go(push(piece, piece, g_feat_send.at[off], g_feat_recv.at[off], {"feat": to}))
    for off in range(1, feats):
        source = lax.rem(f + feats - off, feats)
        piece = result.at[c, p, source]
        push(piece, piece, g_feat_send.at[off], g_feat_recv.at[off], sibling).wait_recv()
    for off in range(1, peers):
        to = lax.rem(p + off, peers)
        piece = result.at[c, p]
        go(push(piece, piece, g_graph_send.at[off], g_graph_recv.at[off], {"graph": to}))
    for off in range(1, peers):
        source = lax.rem(p + peers - off, peers)
        piece = result.at[c, source]
        push(piece, piece, g_graph_send.at[off], g_graph_recv.at[off], sibling).wait_recv()
    go(push(result.at[c], result.at[c], g_sub_send, g_sub_recv, sibling))

    for off in range(1, feats):
        source = lax.rem(f + feats - off, feats)
        push(
            arrived.at[source], arrived.at[source], feat_send.at[off], feat_recv.at[off], sibling
        ).wait_recv()
        own = own + arrived[source].astype(F32)
    node_out[...] = base_ref[...] + dot(own.astype(BF16), w1_ref[width : 2 * width, :], 1, 1)

    other = result.at[1 - c]
    push(other, other, g_sub_send, g_sub_recv, sibling).wait_recv()
    block = result.shape[3]
    e1, e2, n1, n2 = 3 * width, 4 * width, 6 * width, 7 * width
    whole = result[...].reshape(2 * peers * feats * block, width).astype(F32)
    ein_out[...] = whole[:e1] * edge_scale
    eout_out[...] = whole[e1:e2] * edge_scale
    nin_out[...] = whole[e2:n1] * node_scale
    nout_out[...] = whole[n1:n2] * node_scale
    vec_out[0:3, :] = whole[n2 : n2 + 3] * edge_scale
    vec_out[3:6, :] = whole[n2 + 3 : n2 + 6] * node_scale
    for copy in started:
        copy.wait_send()


def reduce(sums, halo_sums, row_lists, terms, base, w1, edge_scale, node_scale):
    slots, nodes, width = sums.shape
    feats = slots // 2
    peers, per = row_lists.shape
    block = terms.shape[0] // (2 * peers * feats)
    vmem = pl.BlockSpec(memory_space=pltpu.VMEM)
    dma = pltpu.SemaphoreType.DMA
    out = [nodes, 3 * width, width, 2 * width, width, 6]
    by_feat = [dma((feats,)), dma((feats,))]
    by_peer = [dma((peers,)), dma((peers,))]
    single = [dma, dma]
    return pl.pallas_call(
        functools.partial(reduce_kernel, peers, feats, edge_scale, node_scale),
        out_shape=tuple(jax.ShapeDtypeStruct((rows, width), F32) for rows in out),
        in_specs=[vmem] * 6,
        out_specs=[vmem] * 6,
        scratch_shapes=[
            pltpu.VMEM((2, peers, feats, block, width), BF16),
            pltpu.VMEM((peers, feats, block, width), BF16),
            pltpu.VMEM((peers, feats, block, width), BF16),
            pltpu.VMEM((feats, block, width), BF16),
            pltpu.VMEM((peers, feats, block, width), BF16),
            pltpu.VMEM((feats, block, width), F32),
            pltpu.VMEM((feats, block, width), BF16),
            pltpu.VMEM((2, peers, feats, block, width), BF16),
            pltpu.VMEM((2, peers, per, width), BF16),
            pltpu.VMEM((feats, nodes, width), BF16),
            pltpu.VMEM((feats, nodes, width), BF16),
            pltpu.VMEM((feats, nodes, width), BF16),
        ]
        + [dma((2, peers)), dma((2, peers))]
        + by_feat
        + by_feat
        + single
        + by_peer
        + by_feat
        + single
        + by_peer
        + by_feat,
        compiler_params=pltpu.CompilerParams(
            collective_id=1, has_side_effects=True, vmem_limit_bytes=32 * 2**20
        ),
    )(
        sums,
        halo_sums,
        row_lists.reshape(1, peers * per),
        terms.reshape(2, peers, feats, block, width),
        base,
        w1,
    )


def per_device(
    node_features,
    edge_features,
    node_cotangent,
    edge_cotangent,
    senders,
    receivers,
    send_rows,
    live_edges,
    *params,
):
    peers = lax.axis_size("graph")
    feats = lax.axis_size("feat")
    row_lists = send_rows[0]
    per = row_lists.shape[1]
    nodes, width = node_features.shape
    unit = 2 * peers * feats * 16
    term_rows = -(-(7 * width + 8) // unit) * unit
    partition, arrived = gather(node_features, row_lists, feats)
    edge_grads, node_base, sums, halo_sums, terms = layer(
        partition,
        arrived.reshape(peers * per, width),
        node_features,
        node_cotangent,
        edge_features,
        edge_cotangent,
        senders,
        receivers,
        live_edges,
        params,
        term_rows,
    )
    device_count = peers * feats * 2
    edge_scale = float(device_count * edge_features.shape[0]) ** (-0.5)
    node_scale = float(device_count * nodes) ** (-0.5)
    node_total, ein, eout, nin, nout, vectors = reduce(
        sums,
        halo_sums.reshape(peers, per, width),
        row_lists,
        terms,
        node_base,
        params[0],
        edge_scale,
        node_scale,
    )
    return (node_total, edge_grads, ein, eout, nin, nout, vectors)


def solution(mesh):
    everywhere = ("groups", "graph", "feat", "sub")
    in_specs = (
        P(everywhere, None),
        P(everywhere, None),
        P(everywhere, None),
        P(everywhere, None),
        P(everywhere),
        P(everywhere),
        P(("groups", "graph"), None, None),
        P(everywhere),
    ) + (P(),) * 9
    out_specs = (
        P(everywhere, None),
        P(everywhere, None),
    ) + (P("groups", None),) * 5
    return jax.shard_map(
        per_device, mesh=mesh, in_specs=in_specs, out_specs=out_specs, check_vma=False
    )
```

```python
import functools

import jax
import jax.numpy as jnp
from jax import lax
from jax.experimental import pallas as pl
from jax.experimental.pallas import tpu as pltpu
from jax.sharding import PartitionSpec as P

epsilon = 1e-05
TILE = 512
F32 = jnp.float32
BF16 = jnp.bfloat16


def dot(a, b, ca=1, cb=0):
    return lax.dot_general(a, b, (((ca,), (cb,)), ((), ())), preferred_element_type=F32)


def sigmoid_of(x):
    return 0.5 * jnp.tanh(0.5 * x) + 0.5


def split(x):
    high = x.astype(BF16)
    low = (x - high.astype(F32)).astype(BF16)
    return jnp.concatenate([high, low], axis=1)


def mean(x):
    return jnp.mean(x, axis=-1, keepdims=True)


def forward(preact, w_out):
    hidden = (preact * sigmoid_of(preact)).astype(BF16)
    output = dot(hidden, w_out)
    centred = output - mean(output)
    inverse = lax.rsqrt(mean(centred * centred) + epsilon)
    return hidden, centred * inverse, inverse


def backward(r, preact, normed, inverse, w_out, gain):
    dn = r * gain
    d_output = inverse * (dn - mean(dn) - normed * mean(dn * normed))
    d_output_b = d_output.astype(BF16)
    d_hidden = dot(d_output_b, w_out, 1, 1)
    sig = sigmoid_of(preact)
    d_preact = d_hidden * sig * (1.0 + preact * (1.0 - sig))
    return d_output_b, d_preact


def down_rows(row):
    width = row.shape[1]
    return jnp.concatenate(
        [jnp.broadcast_to(row[:, c : c + 128], (128, 128)).T for c in range(0, width, 128)], axis=0
    )


def mark(hit):
    return jnp.where(hit, 1.0, 0.0).astype(BF16)


def layer_kernel(
    part_ref,
    halo_ref,
    node_ref,
    ncot_ref,
    ef_ref,
    ec_ref,
    snd_ref,
    rcv_ref,
    live_ref,
    ew1_ref,
    ew2_ref,
    eb_ref,
    eg_ref,
    es_ref,
    nw1_ref,
    nw2_ref,
    nb_ref,
    ng_ref,
    edge_out,
    node_out,
    sums_out,
    halo_out,
    terms_out,
    table,
    pair_table,
    slots_r,
    others,
    preacts,
    hiddens,
    normeds,
    inverses,
    gathered,
    acc,
    acc_rh,
):
    slots, nodes, width = part_ref.shape
    part_rows = slots * nodes
    halos = halo_ref.shape[0]
    rows = table.shape[0]
    groups = part_rows // rows
    tiles = snd_ref.shape[0]
    live = live_ref[0]

    for g in range(groups):
        for k in range(rows // nodes):
            table[k * nodes : (k + 1) * nodes, g * width : (g + 1) * width] = part_ref[
                g * (rows // nodes) + k
            ]
    pair_table[0:nodes, 0:width] = node_ref[...]
    pair_table[0:nodes, width:] = jnp.zeros((nodes, width), BF16)
    pair_table[nodes:, 0:width] = jnp.zeros((halos, width), BF16)
    pair_table[nodes:, width:] = halo_ref[...]
    gathered[...] = jnp.zeros_like(gathered)
    acc[...] = jnp.zeros_like(acc)
    acc_rh[...] = jnp.zeros_like(acc_rh)
    terms_out[...] = jnp.zeros_like(terms_out)

    lane = lax.broadcasted_iota(jnp.int32, (TILE, 128), 1)
    deep = lax.broadcasted_iota(jnp.int32, (TILE, 128), 0)

    def group_of(s):
        group = jnp.zeros_like(s)
        for g in range(1, groups + 1):
            group = group + jnp.where(s >= g * rows, 1, 0)
        return group

    def ahead(i, _):
        here = pl.ds(pl.multiple_of(i * TILE, TILE), TILE)
        snd = snd_ref[i]
        s = down_rows(snd)
        r = down_rows(rcv_ref[i])
        group = group_of(s)
        low = s - group * rows
        far = s - part_rows
        low_hot = jnp.concatenate([mark(low == lane + j) for j in range(0, rows, 128)], axis=1)
        r_hot = jnp.concatenate([mark(r == lane + j) for j in range(0, nodes, 128)], axis=1)
        far_hot = jnp.concatenate([mark(far == lane + j) for j in range(0, halos, 128)], axis=1)
        slots_r[here, :] = r_hot
        picked = dot(low_hot, table[...])
        both = dot(jnp.concatenate([r_hot, far_hot], axis=1), pair_table[...])
        sent = both[:, width:]
        for g in range(groups):
            sent = jnp.where(group == g, picked[:, g * width : (g + 1) * width], sent)
        other = jnp.concatenate([sent.astype(BF16), both[:, :width].astype(BF16)], axis=1)
        others[here, :] = other
        ef = ef_ref[here, :]
        preact = dot(jnp.concatenate([ef, other], axis=1), ew1_ref[...]) + eb_ref[...]
        hidden, normed, inverse = forward(preact, ew2_ref[...])
        preacts[here, :] = preact
        hiddens[here, :] = hidden
        normeds[here, :] = normed
        inverses[here, :] = jnp.broadcast_to(inverse, (TILE, width))
        new = ef.astype(F32) + normed * eg_ref[...] + es_ref[...]
        new = jnp.where(deep + i * TILE < live, new, 0.0)
        gathered[...] += dot(r_hot, split(new), 0, 0)
        return 0

    lax.fori_loop(0, tiles, ahead, 0)

    whole = gathered[:, :width] + gathered[:, width:]
    node_inputs = jnp.concatenate([node_ref[...], whole.astype(BF16)], axis=1)
    preact = dot(node_inputs, nw1_ref[...]) + nb_ref[...]
    hidden, normed, inverse = forward(preact, nw2_ref[...])
    r = ncot_ref[...].astype(F32)
    d_output_b, d_preact = backward(r, preact, normed, inverse, nw2_ref[...], ng_ref[...])
    d_preact_b = d_preact.astype(BF16)
    e1 = 3 * width
    e2 = e1 + width
    n1 = e2 + 2 * width
    n2 = n1 + width
    terms_out[e2:n1, :] = dot(node_inputs, d_preact_b, 0, 0)
    terms_out[n1:n2, :] = dot(hidden, d_output_b, 0, 0)
    terms_out[n2 + 3 : n2 + 4, :] = jnp.sum(d_preact, axis=0, keepdims=True)
    terms_out[n2 + 4 : n2 + 5, :] = jnp.sum(r * normed, axis=0, keepdims=True)
    terms_out[n2 + 5 : n2 + 6, :] = jnp.sum(r, axis=0, keepdims=True)
    d_inputs = dot(d_preact_b, nw1_ref[...], 1, 1)
    node_out[...] = r + d_inputs[:, :width]
    spread = split(d_inputs[:, width:])

    low_deep = lax.broadcasted_iota(jnp.int32, (rows, TILE), 0)
    node_deep = lax.broadcasted_iota(jnp.int32, (nodes, TILE), 0)
    halo_deep = lax.broadcasted_iota(jnp.int32, (halos, TILE), 0)

    def back(i, carried):
        sum_b, sum_g, sum_s = carried
        here = pl.ds(pl.multiple_of(i * TILE, TILE), TILE)
        snd = snd_ref[i]
        rcv = rcv_ref[i]
        group = group_of(snd)
        low_hot = mark(low_deep == snd - group * rows)
        r_hot = mark(node_deep == rcv)
        far_hot = mark(halo_deep == snd - part_rows)
        alive = deep + i * TILE < live
        dg = dot(slots_r[here, :], spread)
        dg = dg[:, :width] + dg[:, width:]
        total = ec_ref[here, :].astype(F32) + jnp.where(alive, dg, 0.0)
        r = jnp.where(alive, total, 0.0)
        normed = normeds[here, :]
        d_output_b, d_preact = backward(
            r, preacts[here, :], normed, inverses[here, :], ew2_ref[...], eg_ref[...]
        )
        d_preact_b = d_preact.astype(BF16)
        edge_out[here, :] = total + dot(d_preact_b, ew1_ref[0:width, :], 1, 1)
        inputs = jnp.concatenate([ef_ref[here, :], others[here, :]], axis=1)
        terms_out[0:e1, :] += dot(inputs, d_preact_b, 0, 0)
        terms_out[e1:e2, :] += dot(hiddens[here, :], d_output_b, 0, 0)
        down = group_of(down_rows(snd))
        zero = jnp.zeros_like(d_preact)
        placed = jnp.concatenate(
            [jnp.where(down == g, d_preact, zero).astype(BF16) for g in range(groups)], axis=1
        )
        acc[...] += dot(low_hot, placed)
        acc_rh[...] += dot(jnp.concatenate([r_hot, far_hot], axis=0), d_preact_b)
        return (
            sum_b + jnp.sum(d_preact, axis=0, keepdims=True),
            sum_g + jnp.sum(r * normed, axis=0, keepdims=True),
            sum_s + jnp.sum(r, axis=0, keepdims=True),
        )

    none = jnp.zeros((1, width), F32)
    sum_b, sum_g, sum_s = lax.fori_loop(0, tiles, back, (none, none, none))
    terms_out[n2 : n2 + 1, :] = sum_b
    terms_out[n2 + 1 : n2 + 2, :] = sum_g
    terms_out[n2 + 2 : n2 + 3, :] = sum_s
    for g in range(groups):
        for k in range(rows // nodes):
            sums_out[g * (rows // nodes) + k] = acc[
                k * nodes : (k + 1) * nodes, g * width : (g + 1) * width
            ].astype(BF16)
    halo_out[...] = acc_rh[nodes:, :].astype(BF16)
    node_out[...] += dot(acc_rh[0:nodes, :].astype(BF16), ew1_ref[2 * width :, :], 1, 1)


def layer(part, halo, node_rows, node_cot, edge_rows, edge_cot, senders, receivers, live, params, terms):
    ew1, ew2, eb, eg, es, nw1, nw2, nb, ng = params
    edges, width = edge_rows.shape
    nodes = node_rows.shape[0]
    halos = halo.shape[0]
    rows = 2 * nodes
    groups = part.shape[0] * part.shape[1] // rows
    tiles = edges // TILE
    eb, eg, es, nb, ng = (v.reshape(1, width) for v in (eb, eg, es, nb, ng))
    vmem = pl.BlockSpec(memory_space=pltpu.VMEM)
    smem = pl.BlockSpec(memory_space=pltpu.SMEM)
    return pl.pallas_call(
        layer_kernel,
        out_shape=(
            jax.ShapeDtypeStruct((edges, width), F32),
            jax.ShapeDtypeStruct((nodes, width), F32),
            jax.ShapeDtypeStruct(part.shape, BF16),
            jax.ShapeDtypeStruct(halo.shape, BF16),
            jax.ShapeDtypeStruct((terms, width), F32),
        ),
        in_specs=[vmem] * 8 + [smem] + [vmem] * 9,
        out_specs=[vmem] * 5,
        scratch_shapes=[
            pltpu.VMEM((rows, groups * width), BF16),
            pltpu.VMEM((nodes + halos, 2 * width), BF16),
            pltpu.VMEM((edges, nodes), BF16),
            pltpu.VMEM((edges, 2 * width), BF16),
            pltpu.VMEM((edges, width), F32),
            pltpu.VMEM((edges, width), BF16),
            pltpu.VMEM((edges, width), F32),
            pltpu.VMEM((edges, width), F32),
            pltpu.VMEM((nodes, 2 * width), F32),
            pltpu.VMEM((rows, groups * width), F32),
            pltpu.VMEM((nodes + halos, width), F32),
        ],
        compiler_params=pltpu.CompilerParams(vmem_limit_bytes=56 * 2**20),
        cost_estimate=pl.CostEstimate(
            flops=2 * edges * width * 10000, bytes_accessed=8 * 2**20, transcendentals=0
        ),
    )(
        part,
        halo,
        node_rows,
        node_cot,
        edge_rows,
        edge_cot,
        senders.reshape(tiles, 1, TILE),
        receivers.reshape(tiles, 1, TILE),
        live,
        ew1,
        ew2,
        eb,
        eg,
        es,
        nw1,
        nw2,
        nb,
        ng,
    )


def greet(partners):
    barrier = pltpu.get_barrier_semaphore()
    for partner in partners:
        pl.semaphore_signal(
            barrier, inc=1, device_id=partner, device_id_type=pl.DeviceIdType.MESH
        )
    pl.semaphore_wait(barrier, len(partners))


def push(src, dst, send, recv, partner):
    return pltpu.make_async_remote_copy(
        src_ref=src,
        dst_ref=dst,
        send_sem=send,
        recv_sem=recv,
        device_id=partner,
        device_id_type=pl.DeviceIdType.MESH,
    )


def around(axis, count):
    me = lax.axis_index(axis)
    return [{axis: lax.rem(me + off, count)} for off in range(1, count)]


def gather_kernel(
    peers, feats, node_ref, rows_ref, part_ref, halo_ref, picked,
    feat_send, feat_recv, sub_send, sub_recv, graph_send, graph_recv
):
    p = lax.axis_index("graph")
    f = lax.axis_index("feat")
    c = lax.axis_index("sub")
    sibling = {"sub": 1 - c}
    nodes = node_ref.shape[0]
    halos = rows_ref.shape[1]
    per = halos // peers
    greet([sibling] + around("feat", feats) + around("graph", peers))
    mine = 2 * f + c
    started = []

    def go(copy):
        copy.start()
        started.append(copy)

    for off in range(feats - 1, 0, -1):
        to = {"feat": lax.rem(f + off, feats)}
        go(push(node_ref, part_ref.at[mine], feat_send.at[off], feat_recv.at[off], to))
    go(push(node_ref, part_ref.at[mine], sub_send.at[0], sub_recv.at[0], sibling))
    part_ref[mine] = node_ref[...]
    for off in range(1, feats):
        source = lax.rem(f + feats - off, feats)
        slot = part_ref.at[2 * source + c]
        push(node_ref, slot, feat_send.at[off], feat_recv.at[off], sibling).wait_recv()
        go(push(slot, slot, sub_send.at[off], sub_recv.at[off], sibling))
    for off in range(feats):
        source = lax.rem(f + feats - off, feats)
        slot = part_ref.at[2 * source + 1 - c]
        push(slot, slot, sub_send.at[off], sub_recv.at[off], sibling).wait_recv()
    deep = lax.broadcasted_iota(jnp.int32, (nodes, halos), 0)
    listed = rows_ref[...]
    chosen = jnp.zeros((halos, node_ref.shape[1]), F32)
    for slot in range(2 * feats):
        chosen = chosen + dot(mark(deep + slot * nodes == listed), part_ref[slot], 0, 0)
    chosen = chosen.astype(BF16)
    for q in range(peers):
        picked[q] = chosen[q * per : (q + 1) * per, :]
    for off in range(1, peers):
        to = lax.rem(p + off, peers)
        go(
            push(
                picked.at[to], halo_ref.at[p], graph_send.at[off], graph_recv.at[off],
                {"graph": to},
            )
        )
    halo_ref[p] = picked[p]
    for off in range(1, peers):
        source = lax.rem(p + peers - off, peers)
        push(
            picked.at[0], halo_ref.at[source], graph_send.at[off], graph_recv.at[off], sibling
        ).wait_recv()
    for copy in started:
        copy.wait_send()


def gather(node_rows, row_lists, feats):
    nodes, width = node_rows.shape
    peers, per = row_lists.shape
    vmem = pl.BlockSpec(memory_space=pltpu.VMEM)
    dma = pltpu.SemaphoreType.DMA
    return pl.pallas_call(
        functools.partial(gather_kernel, peers, feats),
        out_shape=(
            jax.ShapeDtypeStruct((2 * feats, nodes, width), BF16),
            jax.ShapeDtypeStruct((peers, per, width), BF16),
        ),
        in_specs=[vmem] * 2,
        out_specs=[vmem] * 2,
        scratch_shapes=[
            pltpu.VMEM((peers, per, width), BF16),
            dma((feats,)),
            dma((feats,)),
            dma((feats,)),
            dma((feats,)),
            dma((peers,)),
            dma((peers,)),
        ],
        compiler_params=pltpu.CompilerParams(
            collective_id=0, has_side_effects=True, vmem_limit_bytes=32 * 2**20
        ),
    )(node_rows, row_lists.reshape(1, peers * per))


def reduce_kernel(
    peers, feats, edge_scale, node_scale,
    sums_ref, halo_ref, rows_ref, terms_ref, base_ref, w1_ref,
    node_out, ein_out, eout_out, nin_out, nout_out, vec_out,
    narrow, first, second, third, mid, late, onward, result,
    returned, paired, ready, arrived,
    halo_send, halo_recv, pair_send, pair_recv, feat_send, feat_recv,
    t_sub_send, t_sub_recv, t_graph_send, t_graph_recv, t_feat_send, t_feat_recv,
    g_sub_send, g_sub_recv, g_graph_send, g_graph_recv, g_feat_send, g_feat_recv
):
    p = lax.axis_index("graph")
    f = lax.axis_index("feat")
    c = lax.axis_index("sub")
    sibling = {"sub": 1 - c}
    slots, nodes, width = sums_ref.shape
    halos = rows_ref.shape[1]
    per = halos // peers
    across = [{"graph": to["graph"], "sub": 1 - c} for to in around("graph", peers)]
    greet([sibling] + around("feat", feats) + around("graph", peers) + across)
    started = []

    def go(copy):
        copy.start()
        started.append(copy)

    for off in range(1, peers):
        to = lax.rem(p + off, peers)
        for swap, core in enumerate((c, 1 - c)):
            go(
                push(
                    halo_ref.at[to], returned.at[c, p],
                    halo_send.at[swap, off], halo_recv.at[swap, off],
                    {"graph": to, "sub": core},
                )
            )
    go(push(halo_ref.at[p], returned.at[c, p], halo_send.at[1, 0], halo_recv.at[1, 0], sibling))
    narrow[...] = terms_ref[...].astype(BF16)
    go(push(narrow.at[1 - c], first, t_sub_send, t_sub_recv, sibling))
    for off in range(feats - 1, -1, -1):
        to = lax.rem(f + off, feats)
        go(
            push(
                sums_ref.at[2 * to + 1 - c], paired.at[to], pair_send.at[to], pair_recv.at[to],
                sibling,
            )
        )
    returned[c, p] = halo_ref[p]

    push(first, first, t_sub_send, t_sub_recv, sibling).wait_recv()
    mid[...] = (terms_ref[c] + first[...].astype(F32)).astype(BF16)
    for off in range(1, peers):
        to = lax.rem(p + off, peers)
        go(
            push(
                mid.at[to], second.at[p], t_graph_send.at[off], t_graph_recv.at[off],
                {"graph": to},
            )
        )

    for swap, core in enumerate((c, 1 - c)):
        for off in range(1 - swap, peers):
            piece = returned.at[core, lax.rem(p + peers - off, peers)]
            push(
                piece, piece, halo_send.at[swap, off], halo_recv.at[swap, off], sibling
            ).wait_recv()
    boundary = returned[...].reshape(2 * halos, width)
    deep = lax.broadcasted_iota(jnp.int32, (nodes, 2 * halos), 0)
    listed = jnp.concatenate([rows_ref[...], rows_ref[...]], axis=1)

    def joined(owner):
        push(
            paired.at[owner], paired.at[owner], pair_send.at[owner], pair_recv.at[owner], sibling
        ).wait_recv()
        place = 2 * owner + c
        extra = dot(mark(deep + place * nodes == listed), boundary)
        return sums_ref[place].astype(F32) + paired[owner].astype(F32) + extra

    for off in range(feats - 1, 0, -1):
        to = lax.rem(f + off, feats)
        ready[to] = joined(to).astype(BF16)
        go(
            push(
                ready.at[to], arrived.at[f], feat_send.at[off], feat_recv.at[off], {"feat": to}
            )
        )
    own = joined(f)

    total = terms_ref[c, p] + first[p].astype(F32)
    for off in range(1, peers):
        source = lax.rem(p + peers - off, peers)
        push(
            second.at[source], second.at[source], t_graph_send.at[off], t_graph_recv.at[off],
            sibling,
        ).wait_recv()
        total = total + second[source].astype(F32)
    late[...] = total
    onward[...] = total.astype(BF16)
    for off in range(feats - 1, 0, -1):
        to = lax.rem(f + off, feats)
        go(
            push(
                onward.at[to], third.at[f], t_feat_send.at[off], t_feat_recv.at[off],
                {"feat": to},
            )
        )
    total = late[f]
    for off in range(1, feats):
        source = lax.rem(f + feats - off, feats)
        push(
            third.at[source], third.at[source], t_feat_send.at[off], t_feat_recv.at[off], sibling
        ).wait_recv()
        total = total + third[source].astype(F32)
    result[c, p, f] = total.astype(BF16)
    for off in range(1, feats):
        to = lax.rem(f + off, feats)
        piece = result.at[c, p, f]
        go(push(piece, piece, g_feat_send.at[off], g_feat_recv.at[off], {"feat": to}))
    for off in range(1, feats):
        source = lax.rem(f + feats - off, feats)
        piece = result.at[c, p, source]
        push(piece, piece, g_feat_send.at[off], g_feat_recv.at[off], sibling).wait_recv()
    for off in range(1, peers):
        to = lax.rem(p + off, peers)
        piece = result.at[c, p]
        go(push(piece, piece, g_graph_send.at[off], g_graph_recv.at[off], {"graph": to}))
    for off in range(1, peers):
        source = lax.rem(p + peers - off, peers)
        piece = result.at[c, source]
        push(piece, piece, g_graph_send.at[off], g_graph_recv.at[off], sibling).wait_recv()
    go(push(result.at[c], result.at[c], g_sub_send, g_sub_recv, sibling))

    for off in range(1, feats):
        source = lax.rem(f + feats - off, feats)
        push(
            arrived.at[source], arrived.at[source], feat_send.at[off], feat_recv.at[off], sibling
        ).wait_recv()
        own = own + arrived[source].astype(F32)
    node_out[...] = base_ref[...] + dot(own.astype(BF16), w1_ref[width : 2 * width, :], 1, 1)

    other = result.at[1 - c]
    push(other, other, g_sub_send, g_sub_recv, sibling).wait_recv()
    block = result.shape[3]
    e1, e2, n1, n2 = 3 * width, 4 * width, 6 * width, 7 * width
    whole = result[...].reshape(2 * peers * feats * block, width).astype(F32)
    ein_out[...] = whole[:e1] * edge_scale
    eout_out[...] = whole[e1:e2] * edge_scale
    nin_out[...] = whole[e2:n1] * node_scale
    nout_out[...] = whole[n1:n2] * node_scale
    vec_out[0:3, :] = whole[n2 : n2 + 3] * edge_scale
    vec_out[3:6, :] = whole[n2 + 3 : n2 + 6] * node_scale
    for copy in started:
        copy.wait_send()


def reduce(sums, halo_sums, row_lists, terms, base, w1, edge_scale, node_scale):
    slots, nodes, width = sums.shape
    feats = slots // 2
    peers, per = row_lists.shape
    block = terms.shape[0] // (2 * peers * feats)
    vmem = pl.BlockSpec(memory_space=pltpu.VMEM)
    dma = pltpu.SemaphoreType.DMA
    out = [nodes, 3 * width, width, 2 * width, width, 6]
    by_feat = [dma((feats,)), dma((feats,))]
    by_peer = [dma((peers,)), dma((peers,))]
    single = [dma, dma]
    return pl.pallas_call(
        functools.partial(reduce_kernel, peers, feats, edge_scale, node_scale),
        out_shape=tuple(jax.ShapeDtypeStruct((rows, width), F32) for rows in out),
        in_specs=[vmem] * 6,
        out_specs=[vmem] * 6,
        scratch_shapes=[
            pltpu.VMEM((2, peers, feats, block, width), BF16),
            pltpu.VMEM((peers, feats, block, width), BF16),
            pltpu.VMEM((peers, feats, block, width), BF16),
            pltpu.VMEM((feats, block, width), BF16),
            pltpu.VMEM((peers, feats, block, width), BF16),
            pltpu.VMEM((feats, block, width), F32),
            pltpu.VMEM((feats, block, width), BF16),
            pltpu.VMEM((2, peers, feats, block, width), BF16),
            pltpu.VMEM((2, peers, per, width), BF16),
            pltpu.VMEM((feats, nodes, width), BF16),
            pltpu.VMEM((feats, nodes, width), BF16),
            pltpu.VMEM((feats, nodes, width), BF16),
        ]
        + [dma((2, peers)), dma((2, peers))]
        + by_feat
        + by_feat
        + single
        + by_peer
        + by_feat
        + single
        + by_peer
        + by_feat,
        compiler_params=pltpu.CompilerParams(
            collective_id=1, has_side_effects=True, vmem_limit_bytes=32 * 2**20
        ),
    )(
        sums,
        halo_sums,
        row_lists.reshape(1, peers * per),
        terms.reshape(2, peers, feats, block, width),
        base,
        w1,
    )


def per_device(
    node_features,
    edge_features,
    node_cotangent,
    edge_cotangent,
    senders,
    receivers,
    send_rows,
    live_edges,
    *params,
):
    peers = lax.axis_size("graph")
    feats = lax.axis_size("feat")
    row_lists = send_rows[0]
    per = row_lists.shape[1]
    nodes, width = node_features.shape
    unit = 2 * peers * feats * 16
    term_rows = -(-(7 * width + 8) // unit) * unit
    partition, arrived = gather(node_features, row_lists, feats)
    edge_grads, node_base, sums, halo_sums, terms = layer(
        partition,
        arrived.reshape(peers * per, width),
        node_features,
        node_cotangent,
        edge_features,
        edge_cotangent,
        senders,
        receivers,
        live_edges,
        params,
        term_rows,
    )
    device_count = peers * feats * 2
    edge_scale = float(device_count * edge_features.shape[0]) ** (-0.5)
    node_scale = float(device_count * nodes) ** (-0.5)
    node_total, ein, eout, nin, nout, vectors = reduce(
        sums,
        halo_sums.reshape(peers, per, width),
        row_lists,
        terms,
        node_base,
        params[0],
        edge_scale,
        node_scale,
    )
    return (node_total, edge_grads, ein, eout, nin, nout, vectors)


def solution(mesh):
    everywhere = ("groups", "graph", "feat", "sub")
    in_specs = (
        P(everywhere, None),
        P(everywhere, None),
        P(everywhere, None),
        P(everywhere, None),
        P(everywhere),
        P(everywhere),
        P(("groups", "graph"), None, None),
        P(everywhere),
    ) + (P(),) * 9
    out_specs = (
        P(everywhere, None),
        P(everywhere, None),
    ) + (P("groups", None),) * 5
    return jax.shard_map(
        per_device, mesh=mesh, in_specs=in_specs, out_specs=out_specs, check_vma=False
    )
```
